32 devices in a mesh: pipe: 8 (over z, y), expert: 4 (over x, core).
Axes of the slice: x: 2, y: 2, z: 4, core: 2. Of those that a mesh axis runs over, the one named last changes fastest.
Arguments:
- saved: bfloat16 [2, 512, 6144], P(None, 'expert', 'pipe'), may hold values from -6 to 6
- top_grad: bfloat16 [2, 512, 6144], P(None, 'expert', 'pipe'), may hold values from -6 to 6
- norm_gain: float32 [6144], P('pipe'), may hold values from 0.1 to 1.9
- w_gate: bfloat16 [4, 6144, 8192], P('expert', None, 'pipe'), may hold values from -0.078125 to 0.078125
- w_up: bfloat16 [4, 6144, 8192], P('expert', None, 'pipe'), may hold values from -0.078125 to 0.078125
- w_down: bfloat16 [4, 8192, 6144], P('expert', 'pipe'), may hold values from -0.0625 to 0.0625
- routes: int32 [2, 512, 2], P(None, 'expert'), may hold values from 0 to 3, all different within a row; in each aligned block of 128 rows (0 to 127, 128 to 255, ..., all dimensions but the last counted through in order) at most 96 rows name the same one
- gates: float32 [2, 512, 2], P(None, 'expert'), may hold values from 0.1 to 0.9
Outputs:
- input_grads: float32 [2, 512, 6144], P(None, 'expert', 'pipe')
- grad_gain: float32 [6144], P('pipe')
The draws below stay inside these ranges and needn't reach their ends.
Inputs may be any that keep to these rules, and one draw needn't show every extreme that they name: `routes`: each token names two different experts; in every aligned block of 128 rows of one micro-batch no expert is named more than 96 times, a bound that some block reaches.
All inputs are finite; a program needn't handle non-finite values.
Results may differ from the reference program's by a relative error of at most 0.017.
Values may be sent and summed in bfloat16 or wider, within the bound.
A program may use at most 128 MiB of HBM per device.

```python
import math
import jax
import jax.numpy as jnp
import numpy as np
from jax import lax

D = 6144
EXPERTS = 4
FF = 8192
FF_DEV = 1024
MB = 2
TOK_DEV = 128
TOKENS = 512
CAP = 96
N_PIPE = 8
N_EXPERT = 4


def steps_of(stream_key, extent, shards, low, largest):
    def one(dim, shards_of):
        steps = jax.random.uniform(jax.random.fold_in(jax.random.fold_in(stream_key, 6), dim), (shards_of,), jnp.float32, low / len(shards), largest / len(shards))
        return jnp.repeat(jnp.exp(steps), extent[dim] // shards_of).reshape((-1,) + (1,) * (len(extent) - dim - 1))

    level = one(*shards[0])
    for cut in shards[1:]:
        level = level * one(*cut)
    return level


def routed_block(own_key, own, number, rows, amount, top, most, skew):
    sequence = jax.random.permutation(own_key, amount)
    packed, common = load_shares(amount, rows * top, most, skew, True), load_shares(amount, rows * top, most, skew, False)
    places = jnp.arange(amount)

    def named(sizes, offset_by):
        used = int((sizes > 0).sum())
        fixed = max(1, used // 4)
        moved = fixed + (places - fixed + offset_by * (used - fixed)) % max(1, amount - fixed)
        return jnp.zeros((amount,), jnp.int32).at[sequence[jnp.where(places < fixed, places, moved)]].set(jnp.asarray(sizes, jnp.int32))

    sizes = jnp.where(number % 4 == 0, named(packed, number // 4), named(common, number - number // 4 - 1))
    mixed = jax.random.permutation(jax.random.fold_in(own, 3), amount)
    donor, receiver = mixed[0:amount // 2 * 2:2], mixed[1:amount // 2 * 2:2]
    room = jnp.minimum(sizes[donor] - 1, most - sizes[receiver]) // 2
    room = jnp.where((donor == sequence[0]) | (receiver == sequence[0]) | (sizes[receiver] == 0), 0, jnp.maximum(room, 0))
    moved = jax.random.randint(jax.random.fold_in(own, 4), (amount // 2,), 0, 1 << 20) % (room + 1)
    sizes = sizes.at[donor].add(-moved).at[receiver].add(moved)
    items = jnp.searchsorted(jnp.cumsum(sizes), jnp.arange(rows * top), side="right").astype(jnp.int32)
    grid = items.reshape(top, rows).T
    grid = grid[jax.random.permutation(jax.random.fold_in(own, 1), rows)]
    offset_by = jax.random.randint(jax.random.fold_in(own, 2), (rows, 1), 0, top)
    return jnp.take_along_axis(grid, (jnp.arange(top)[None, :] + offset_by) % top, axis=1)


def load_shares(amount, total, bound, skew, full):
    portions = [(1 << 20) // math.isqrt(standing ** skew) + 1 for standing in range(1, amount + 1)]
    largest = bound if full else min(bound, max(-(-total // amount), total * portions[0] // sum(portions)))
    least = 1 if total - largest >= amount - 1 else 0
    holding, spare = [largest] + [least] * (amount - 1), total - largest - least * (amount - 1)
    while spare > 0:
        free = [i for i in range(1, amount) if holding[i] < largest] or [i for i in range(1, amount) if holding[i] < bound]
        whole, budget = sum([portions[i] for i in free]), spare
        for i in free:
            more = min(bound - holding[i], max(1, budget * portions[i] // whole), spare)
            holding[i] = holding[i] + more
            spare = spare - more
    return np.array(holding)


def normal_values(key, shape, scale, limit, split=(), kind=jnp.bfloat16):
    entries = jax.random.normal(key, shape, jnp.float32) * scale
    if len(split) > 0:
        entries = steps_of(key, shape, split, -0.22, 0.18) * entries
    return jnp.clip(entries, min=-limit, max=limit).astype(kind)


def setup_inputs(seed: int = 0) -> dict:
    key_of = jax.random.split(jax.random.key(seed), 9)
    saved = normal_values(key_of[0], (MB, TOKENS, D), 1.0, 6.0, ((1, 4), (2, 8)))
    top_grad = normal_values(key_of[1], (MB, TOKENS, D), 1.0, 6.0, ((1, 4), (2, 8)))
    norm_gain = jnp.clip(1.0 + 0.18 * jax.random.normal(key_of[2], (D,), jnp.float32), 0.1, 1.9)
    w_gate = normal_values(key_of[3], (EXPERTS, D, FF), D ** -0.5, 0.078125, ((0, 4), (2, 8)))
    w_up = normal_values(key_of[4], (EXPERTS, D, FF), D ** -0.5, 0.078125, ((0, 4), (2, 8)))
    w_down = normal_values(key_of[5], (EXPERTS, FF, D), FF ** -0.5, 0.0625, ((0, 4), (1, 8)))
    routes_keys = jax.random.split(jax.random.fold_in(key_of[6], 1), MB * TOKENS // TOK_DEV)
    routes_turns = jax.random.permutation(jax.random.fold_in(key_of[6], 3), MB * TOKENS // TOK_DEV)
    routes = jax.vmap(lambda own, number: routed_block(jax.random.fold_in(key_of[6], 2), own, number, TOK_DEV, EXPERTS, 2, CAP, 2))(routes_keys, routes_turns).reshape((MB, TOKENS, 2))
    gates = jnp.clip(0.1 + 0.79999997 * jax.random.uniform(key_of[7], (MB, TOKENS, 2), jnp.float32) ** steps_of(key_of[7], (MB, TOKENS, 2), ((1, 4),), -0.2, 0.2), 0.1, 0.9)
    return {"saved": saved, "top_grad": top_grad, "norm_gain": norm_gain, "w_gate": w_gate, "w_up": w_up, "w_down": w_down, "routes": routes, "gates": gates}


eps = 1e-05

def expert_rows(item):
    rows_x, rows_g, wg, wu, down_weight = item
    pre_a = jnp.dot(rows_x, wg, preferred_element_type=jnp.float32)
    pre_b = jnp.dot(rows_x, wu, preferred_element_type=jnp.float32)
    d_hidden = jnp.dot(rows_g, down_weight.T, preferred_element_type=jnp.float32)
    sig = jax.nn.sigmoid(pre_a)
    act = pre_a * sig
    d_a = (d_hidden * pre_b * sig * (1.0 + pre_a * (1.0 - sig))).astype(jnp.bfloat16)
    d_b = (d_hidden * act).astype(jnp.bfloat16)
    count = rows_x.shape[0]
    split_a = d_a.reshape(count, N_PIPE, FF_DEV).transpose(1, 0, 2)
    split_b = d_b.reshape(count, N_PIPE, FF_DEV).transpose(1, 0, 2)
    split_g = wg.reshape(D, N_PIPE, FF_DEV).transpose(1, 0, 2)
    split_u = wu.reshape(D, N_PIPE, FF_DEV).transpose(1, 0, 2)

    def add(total, group):
        part_a, part_b, part_g, part_u = group
        partial_value = jnp.dot(part_a, part_g.T, preferred_element_type=jnp.float32)
        partial_value = partial_value + jnp.dot(part_b, part_u.T, preferred_element_type=jnp.float32)
        partial_value = lax.optimization_barrier(partial_value.astype(jnp.bfloat16)).astype(jnp.float32)
        return (total + partial_value, None)
    total, unused = lax.scan(add, jnp.zeros((count, D), jnp.float32), (split_a, split_b, split_g, split_u))
    return total.astype(jnp.bfloat16)

def reference(saved, top_grad, norm_gain, w_gate, w_up, w_down, routes, gates):
    grads = []
    gain_total = jnp.zeros((D,), jnp.float32)
    for batch in range(MB):
        xf = saved[batch].astype(jnp.float32)
        dy = top_grad[batch].astype(jnp.float32)
        scale = lax.rsqrt(lax.optimization_barrier(jnp.mean(xf * xf, axis=-1, keepdims=True)) + eps)
        normed = (xf * scale * norm_gain).astype(jnp.bfloat16)
        blocks = routes[batch].reshape(N_EXPERT, 2 * TOK_DEV)
        onehot = (blocks[:, :, None] == jnp.arange(EXPERTS, dtype=jnp.int32)[None, None, :]).astype(jnp.int32)
        before = jnp.cumsum(onehot, axis=1) - onehot
        slot = lax.optimization_barrier(jnp.sum(before * onehot, axis=-1)).astype(jnp.int32)
        source = jnp.arange(N_EXPERT, dtype=jnp.int32)[:, None]
        target = (blocks * (N_EXPERT * CAP) + source * CAP + slot).reshape(-1).astype(jnp.int32)
        pairs = jnp.repeat(normed, 2, axis=0)
        rows_x = jnp.zeros((EXPERTS * N_EXPERT * CAP, D), normed.dtype).at[target].set(pairs)
        pair_grad = (gates[batch][:, :, None] * dy[:, None, :]).reshape(2 * TOKENS, D).astype(jnp.bfloat16)
        rows_g = jnp.zeros((EXPERTS * N_EXPERT * CAP, D), pair_grad.dtype).at[target].set(pair_grad)
        d_rows = lax.map(expert_rows, (rows_x.reshape(EXPERTS, N_EXPERT * CAP, D), rows_g.reshape(EXPERTS, N_EXPERT * CAP, D), w_gate, w_up, w_down))
        d_pairs = d_rows.reshape(EXPERTS * N_EXPERT * CAP, D)[target].astype(jnp.float32)
        d_norm = d_pairs.reshape(TOKENS, 2, D).sum(axis=1)
        gain_total = gain_total + lax.optimization_barrier(jnp.sum(d_norm * xf * scale, axis=0))
        scaled = norm_gain * d_norm
        d_x = scale * scaled - xf * scale ** 3 * lax.optimization_barrier(jnp.mean(scaled * xf, axis=-1, keepdims=True))
        grads.append(dy + d_x)
    return (jnp.stack(grads), gain_total)
```

```python
import jax
import jax.numpy as jnp
from jax import lax
from jax.sharding import PartitionSpec as P

eps = 1e-05
CORES = 2


def rows_dot(left, right):
    return lax.dot_general(
        left, right, (((1,), (0,)), ((), ())), preferred_element_type=jnp.float32
    )


def contract_last(left, right):
    return lax.dot_general(
        left, right, (((1,), (1,)), ((), ())), preferred_element_type=jnp.float32
    )


def body(saved, top_grad, norm_gain, w_gate, w_up, w_down, routes, gates):
    n_pipe = lax.axis_size("pipe")
    n_experts = lax.axis_size("expert")
    n_x = n_experts // CORES
    micro, tok, part = saved.shape
    width = part * n_pipe
    wg, wu, wd = w_gate[0], w_up[0], w_down[0]
    expert = lax.axis_index("expert")

    def index(x, core):
        return (x % n_x) * CORES + core

    def across(value, shift):
        pairs = [(index(x + shift, c), index(x, c)) for x in range(n_x) for c in range(CORES)]
        return lax.ppermute(value, "expert", pairs)

    def sibling(value):
        return lax.ppermute(value, "expert", [(i, i ^ 1) for i in range(n_experts)])

    inputs = saved.astype(jnp.float32)
    upstream = top_grad.astype(jnp.float32)

    gained = (inputs * norm_gain).astype(jnp.bfloat16).reshape(micro * tok, part)
    mine = lax.all_gather(gained, "pipe", axis=1, tiled=True)
    grads = top_grad.reshape(micro * tok, part)
    grads = jnp.concatenate([grads] + [across(grads, k) for k in range(1, n_x)], axis=0)
    grads = lax.all_gather(grads, "pipe", axis=1, tiled=True)
    own_x = [mine] + [across(mine, k) for k in range(1, n_x)]
    x_rows = [(value, sibling(value)) for value in own_x]
    g_rows = (grads, sibling(grads))

    squares = lax.psum(jnp.sum(inputs * inputs, axis=-1), "pipe")
    scale = lax.rsqrt(squares / width + eps)
    facts = jnp.concatenate(
        [scale[None], jnp.moveaxis(gates, 2, 0), jnp.moveaxis(routes, 2, 0).astype(jnp.float32)],
        axis=0,
    ).reshape(5, micro * tok)
    facts = lax.all_gather(facts, "expert", axis=0)
    chip, core = expert // CORES, expert % CORES
    named = expert.astype(jnp.float32)

    def block_facts(k, flip):
        source = ((chip + k) % n_x) * CORES + jnp.where(flip, 1 - core, core)
        block = lax.dynamic_index_in_dim(facts, source, 0, keepdims=False)
        gate = jnp.where(block[3] == named, block[1], 0.0) + jnp.where(
            block[4] == named, block[2], 0.0
        )
        return block[0][:, None], gate[:, None]

    span = micro * tok
    hidden_grads = {}
    for flip in range(CORES):
        d_hidden_all = contract_last(g_rows[flip], wd)
        for k in range(n_x):
            row_scale, row_gate = block_facts(k, flip)
            pre_a = rows_dot(x_rows[k][flip], wg) * row_scale
            pre_b = rows_dot(x_rows[k][flip], wu) * row_scale
            d_hidden = d_hidden_all[k * span : (k + 1) * span] * row_gate
            sig = jax.nn.sigmoid(pre_a)
            d_a = (d_hidden * pre_b * sig * (1.0 + pre_a * (1.0 - sig))).astype(jnp.bfloat16)
            d_b = (d_hidden * (pre_a * sig)).astype(jnp.bfloat16)
            hidden_grads[flip, k] = (d_a, d_b)

    def back(flip, m):
        pieces = [
            tuple(v[m * tok : (m + 1) * tok] for v in hidden_grads[flip, k]) for k in range(n_x)
        ]
        left = jnp.concatenate([a for a, b in pieces], axis=0)
        right = jnp.concatenate([b for a, b in pieces], axis=0)
        return contract_last(wg, left) + contract_last(wu, right)

    def scatter(value):
        return lax.psum_scatter(value, "pipe", scatter_dimension=0, tiled=True)

    others = [sibling(back(1, m).astype(jnp.bfloat16)) for m in reversed(range(micro))][::-1]
    norms = [None] * micro
    for m in reversed(range(micro)):
        chip_sum = back(0, m) + others[m].astype(jnp.float32)
        if m == 0 and micro > 1:
            total = chip_sum[:, :tok]
            for k in range(1, n_x):
                piece = chip_sum[:, k * tok : (k + 1) * tok].astype(jnp.bfloat16)
                total = total + across(piece, n_x - k).astype(jnp.float32)
            norms[m] = scatter(total.astype(jnp.bfloat16)).astype(jnp.float32)
        else:
            reduced = scatter(chip_sum.astype(jnp.bfloat16))
            total = reduced[:, :tok].astype(jnp.float32)
            for k in range(1, n_x):
                total = total + across(reduced[:, k * tok : (k + 1) * tok], n_x - k).astype(
                    jnp.float32
                )
            norms[m] = total
    d_norm = jnp.stack([value.T for value in norms], axis=0)
    scale = scale[:, :, None]
    scaled = norm_gain * d_norm
    inner = lax.psum(jnp.sum(scaled * inputs, axis=-1), "pipe")
    d_x = scale * scaled - inputs * scale**3 * (inner / width)[:, :, None]
    input_grads = upstream + d_x
    gain_part = jnp.sum(d_norm * inputs * scale, axis=(0, 1))
    grad_gain = lax.psum(gain_part, "expert")
    return (input_grads, grad_gain)


def solution(mesh):
    placed = (
        P(None, "expert", "pipe"),
        P(None, "expert", "pipe"),
        P("pipe"),
        P("expert", None, "pipe"),
        P("expert", None, "pipe"),
        P("expert", "pipe", None),
        P(None, "expert", None),
        P(None, "expert", None),
    )
    return jax.shard_map(
        body,
        mesh=mesh,
        in_specs=placed,
        out_specs=(P(None, "expert", "pipe"), P("pipe")),
        check_vma=False,
    )
```

```python
import jax
import jax.numpy as jnp
from jax import lax
from jax.sharding import PartitionSpec as P

eps = 1e-05
CORES = 2


def rows_dot(left, right):
    return lax.dot_general(
        left, right, (((1,), (0,)), ((), ())), preferred_element_type=jnp.float32
    )


def contract_last(left, right):
    return lax.dot_general(
        left, right, (((1,), (1,)), ((), ())), preferred_element_type=jnp.float32
    )


def body(saved, top_grad, norm_gain, w_gate, w_up, w_down, routes, gates):
    n_pipe = lax.axis_size("pipe")
    n_experts = lax.axis_size("expert")
    n_x = n_experts // CORES
    micro, tok, part = saved.shape
    width = part * n_pipe
    wg, wu, wd = w_gate[0], w_up[0], w_down[0]
    expert = lax.axis_index("expert")

    def index(x, core):
        return (x % n_x) * CORES + core

    def across(value, shift):
        pairs = [(index(x + shift, c), index(x, c)) for x in range(n_x) for c in range(CORES)]
        return lax.ppermute(value, "expert", pairs)

    def sibling(value):
        return lax.ppermute(value, "expert", [(i, i ^ 1) for i in range(n_experts)])

    inputs = saved.astype(jnp.float32)
    upstream = top_grad.astype(jnp.float32)

    gained = (inputs * norm_gain).astype(jnp.bfloat16).reshape(micro * tok, part)
    mine = lax.all_gather(gained, "pipe", axis=1, tiled=True)
    grads = top_grad.reshape(micro * tok, part)
    grads = jnp.concatenate([grads] + [across(grads, k) for k in range(1, n_x)], axis=0)
    grads = lax.all_gather(grads, "pipe", axis=1, tiled=True)
    squares = lax.psum(jnp.sum(inputs * inputs, axis=-1), "pipe")
    scale = lax.rsqrt(squares / width + eps)
    facts = jnp.concatenate(
        [scale[None], jnp.moveaxis(gates, 2, 0), jnp.moveaxis(routes, 2, 0).astype(jnp.float32)],
        axis=0,
    ).reshape(5, micro * tok)
    facts = lax.all_gather(facts, "expert", axis=0)
    mine, facts = lax.optimization_barrier((mine, facts))
    own_x = [mine] + [across(mine, k) for k in range(1, n_x)]
    x_rows = [(value, sibling(value)) for value in own_x]
    chip, core = expert // CORES, expert % CORES
    named = expert.astype(jnp.float32)

    def block_facts(k, flip):
        source = ((chip + k) % n_x) * CORES + jnp.where(flip, 1 - core, core)
        block = lax.dynamic_index_in_dim(facts, source, 0, keepdims=False)
        gate = jnp.where(block[3] == named, block[1], 0.0) + jnp.where(
            block[4] == named, block[2], 0.0
        )
        return block[0][:, None], gate[:, None]

    span = micro * tok
    pieces = [(flip, k) for flip in range(CORES) for k in range(n_x)]
    gate_pre = [rows_dot(x_rows[k][flip], wg) for flip, k in pieces]
    up_pre = [rows_dot(x_rows[k][flip], wu) for flip, k in pieces]
    grads, gate_pre, up_pre = lax.optimization_barrier((grads, gate_pre, up_pre))
    g_rows = (grads, sibling(grads))
    d_hidden_all = [contract_last(rows, wd) for rows in g_rows]
    hidden_grads = {}
    for (flip, k), pre_a, pre_b in zip(pieces, gate_pre, up_pre):
        row_scale, row_gate = block_facts(k, flip)
        pre_a, pre_b = pre_a * row_scale, pre_b * row_scale
        d_hidden = d_hidden_all[flip][k * span : (k + 1) * span] * row_gate
        sig = jax.nn.sigmoid(pre_a)
        d_a = (d_hidden * pre_b * sig * (1.0 + pre_a * (1.0 - sig))).astype(jnp.bfloat16)
        d_b = (d_hidden * (pre_a * sig)).astype(jnp.bfloat16)
        hidden_grads[flip, k] = (d_a, d_b)

    order = [
        tuple(v[m * tok : (m + 1) * tok] for v in hidden_grads[flip, k])
        for flip in reversed(range(CORES))
        for m in range(micro)
        for k in range(n_x)
    ]
    left = jnp.concatenate([a for a, b in order], axis=0)
    right = jnp.concatenate([b for a, b in order], axis=0)
    back = contract_last(wg, left) + contract_last(wu, right)
    half = n_x * span
    block = n_x * tok
    kept = back[:, half:]
    others = [
        sibling(back[:, m * block : (m + 1) * block].astype(jnp.bfloat16)) for m in range(micro)
    ]

    def scatter(value):
        return lax.psum_scatter(value, "pipe", scatter_dimension=0, tiled=True)

    norms = [None] * micro
    for m in reversed(range(micro)):
        chip_sum = kept[:, m * block : (m + 1) * block] + others[m].astype(jnp.float32)
        if m == 0 and micro > 1:
            total = chip_sum[:, :tok]
            for k in range(1, n_x):
                piece = chip_sum[:, k * tok : (k + 1) * tok].astype(jnp.bfloat16)
                total = total + across(piece, n_x - k).astype(jnp.float32)
            norms[m] = scatter(total.astype(jnp.bfloat16)).astype(jnp.float32)
        else:
            reduced = scatter(chip_sum.astype(jnp.bfloat16))
            total = reduced[:, :tok].astype(jnp.float32)
            for k in range(1, n_x):
                total = total + across(reduced[:, k * tok : (k + 1) * tok], n_x - k).astype(
                    jnp.float32
                )
            norms[m] = total
    d_norm = jnp.stack([value.T for value in norms], axis=0)
    scale = scale[:, :, None]
    scaled = norm_gain * d_norm
    inner = lax.psum(jnp.sum(scaled * inputs, axis=-1), "pipe")
    d_x = scale * scaled - inputs * scale**3 * (inner / width)[:, :, None]
    input_grads = upstream + d_x
    gain_part = jnp.sum(d_norm * inputs * scale, axis=(0, 1))
    grad_gain = lax.psum(gain_part, "expert")
    return (input_grads, grad_gain)


def solution(mesh):
    placed = (
        P(None, "expert", "pipe"),
        P(None, "expert", "pipe"),
        P("pipe"),
        P("expert", None, "pipe"),
        P("expert", None, "pipe"),
        P("expert", "pipe", None),
        P(None, "expert", None),
        P(None, "expert", None),
    )
    return jax.shard_map(
        body,
        mesh=mesh,
        in_specs=placed,
        out_specs=(P(None, "expert", "pipe"), P("pipe")),
        check_vma=False,
    )
```
